32 devices in a mesh: groups: 2 (over y), seq: 4 (over z), head: 2 (over x), tp: 2 (over core).
Axes of the slice: x: 2, y: 2, z: 4, core: 2. Of those that a mesh axis runs over, the one named last changes fastest.
Arguments:
- ssm_input: bfloat16 [2048, 8192], P(('groups', 'seq'), ('head', 'tp')), parts along dimension 0, may hold values from -6 to 6
- ssm_gate: bfloat16 [2048, 8192], P(('groups', 'seq'), ('head', 'tp')), parts along dimension 0, may hold values from -6 to 6
- input_map: bfloat16 [2048, 512], P(('groups', 'seq'), ('head', 'tp')), parts along dimension 0, may hold values from -0.5 to 0.5
- output_map: bfloat16 [2048, 512], P(('groups', 'seq'), ('head', 'tp')), parts along dimension 0, may hold values from -6 to 6
- step_size: float32 [128, 2048], P(('head', 'tp'), ('groups', 'seq')), parts along dimension 1, may hold values from 0.5 to 2
- decay_log: float32 [128], P(('head', 'tp')), may hold values from -16 to -2
- skip_gain: float32 [128], P(('head', 'tp')), may hold values from 0.5 to 1.5
- norm_gain: float32 [8192], P(('head', 'tp')), may hold values from 0.25 to 1.75
- doc_lengths: int32 [8], P('groups'), parts along dimension 0, may hold values from 1 to 512, 1024 in all
- queries: bfloat16 [2048, 4096], P(('groups', 'seq', 'head'), 'tp'), parts along dimension 0, may hold values from -64 to 64
- keys_in: bfloat16 [2048, 1024], P(('groups', 'seq', 'head'), 'tp'), parts along dimension 0, may hold values from -16 to 16
- values_in: bfloat16 [2048, 1024], P(('groups', 'seq', 'head'), 'tp'), parts along dimension 0, may hold values from -6 to 6
Outputs:
- ssm_out: bfloat16 [2048, 8192], P(('groups', 'seq'), ('head', 'tp')), parts along dimension 0
- attn_out: bfloat16 [2048, 4096], P(('groups', 'seq', 'head'), 'tp'), parts along dimension 0
The draws below stay inside these ranges and needn't reach their ends.
There are 2 independent parts, one for each index of `groups`. The reference program is written for one: setup_inputs(seed, part) draws one part's arguments, and reference() takes and returns one part's arrays. A program takes and returns all parts, laid end to end along the dimension named above; an argument that names none is the same for every part. Nothing has to cross between parts.
Inputs may be any that keep to these rules, and one draw needn't show every extreme that they name: `doc_lengths`: the 4 documents lie end to end from position 0; their lengths sum to 1024.
All inputs are finite; a program needn't handle non-finite values.
Results may differ from the reference program's by a relative error of at most 0.0052.
Values may be sent and summed in bfloat16 or wider, within the bound.
A program may use at most 128 MiB of HBM per device.

```python
import math
import jax
import jax.numpy as jnp
import numpy as np
from jax import lax

TOK_DEV = 128
MHEADS = 128
HEAD_P = 64
STATE = 128
QHEADS = 32
KVHEADS = 8
HEAD_D = 128
REACH = 2
GROUPS = 4
TOKENS = 1024
DOC_MAX = 512
NDOCS = 4
N_HEAD = 2
N_TP = 2


def draw_keys_in(key, part):
    drawn_draw = jax.random.normal(jax.random.fold_in(key, 21), (TOKENS, KVHEADS * HEAD_D), jnp.float32)
    drawn_draw = jnp.clip(drawn_draw, -4.0, 4.0)
    return drawn_draw.astype(jnp.bfloat16)


def draw_queries(key, part):
    drawn_draw = jax.random.normal(jax.random.fold_in(key, 22), (TOKENS, QHEADS * HEAD_D), jnp.float32)
    drawn_draw = jnp.clip(drawn_draw, -4.0, 4.0)
    return drawn_draw.astype(jnp.bfloat16)


def draw_decay_log(key, part):
    fast_share = 0.5
    fast_pick = jax.random.uniform(jax.random.fold_in(key, 41), (MHEADS,), jnp.float32) < fast_share
    fast_rate = jax.random.uniform(jax.random.fold_in(key, 42), (MHEADS,), jnp.float32, math.log(0.02), math.log(0.1))
    slow_rate = jax.random.uniform(jax.random.fold_in(key, 43), (MHEADS,), jnp.float32, math.log(0.1 / DOC_MAX), math.log(1.5 / DOC_MAX))
    return jnp.where(fast_pick, fast_rate, slow_rate)


def level_of(stream_key, extent, split, smallest, largest):
    gain, own = 1.0, jax.random.fold_in(stream_key, 6)
    for dim, shards_of in split:
        steps = jnp.exp(jax.random.uniform(jax.random.fold_in(own, dim), (shards_of,), jnp.float32, smallest / len(split), largest / len(split)))
        gain = gain * jnp.repeat(steps, extent[dim] // shards_of).reshape([-1 if axis == dim else 1 for axis in range(len(extent))])
    return gain


def profile(number_of, total, bound, skew):
    portions = [(1 << 20) // math.isqrt(standing ** skew) + 1 for standing in range(2, number_of + 1)]
    surplus, holding = total - bound - (number_of - 1), [1] * (number_of - 1)
    while surplus > 0:
        candidates = [i for i in range(number_of - 1) if holding[i] < bound]
        pool, remaining = sum([portions[i] for i in candidates]), surplus
        for i in candidates:
            more = min(bound - holding[i], max(1, remaining * portions[i] // pool), surplus)
            holding[i] = holding[i] + more
            surplus = surplus - more
    return np.array([bound] + holding)


def uneven_parts(rng, number_of, total, bound, lean):
    if number_of == 2:
        one = jax.random.randint(rng, (), max(1, total - bound), min(bound, total - 1) + 1)
        return jnp.stack([one, total - one])
    lengths = jnp.asarray(profile(number_of, total, bound, lean), jnp.int32)
    twos = (number_of - 1) // 2
    source_of, receiver = lengths[1:1 + 2 * twos:2], lengths[2:2 + 2 * twos:2]
    room = jnp.minimum(source_of - 1, bound - receiver)
    moved = jax.random.randint(jax.random.fold_in(rng, 1), (twos,), 0, 1 << 20) % (room + 1)
    lengths = lengths.at[1:1 + 2 * twos:2].set(source_of - moved).at[2:2 + 2 * twos:2].set(receiver + moved)
    return lengths[jax.random.permutation(jax.random.fold_in(rng, 2), number_of)]


def normal_values(own_key, shape, scale, bound, shards=(), kind=jnp.bfloat16):
    values = scale * jax.random.normal(own_key, shape, jnp.float32)
    if shards:
        values = values * level_of(own_key, shape, shards, -0.22, 0.18)
    return jnp.clip(values, -bound, bound).astype(kind)


def setup_inputs(seed: int = 0, part: int = 0) -> dict:
    keys = jax.random.split(jax.random.key(seed), 13)
    own_keys = jax.random.split(jax.random.fold_in(keys[12], part), 13)
    return {
        "ssm_input": normal_values(own_keys[0], (TOKENS, MHEADS * HEAD_P), 1.0, 6.0, ((0, 4), (1, 4))),
        "ssm_gate": normal_values(own_keys[1], (TOKENS, MHEADS * HEAD_P), 1.0, 6.0, ((0, 4), (1, 4))),
        "input_map": normal_values(own_keys[2], (TOKENS, GROUPS * STATE), STATE ** -0.5, 0.5, ((0, 4), (1, 4))),
        "output_map": normal_values(own_keys[3], (TOKENS, GROUPS * STATE), 1.0, 6.0, ((0, 4), (1, 4))),
        "step_size": jnp.clip(jnp.exp(math.log(2.0) - 1.3862944 * jax.random.uniform(own_keys[4], (MHEADS, TOKENS), jnp.float32) ** level_of(own_keys[4], (MHEADS, TOKENS), ((0, 4), (1, 4)), -0.2, 0.2)), 0.5, 2.0),
        "decay_log": draw_decay_log(jax.random.fold_in(keys[12], 71), part),
        "skip_gain": jnp.clip(0.5 + 1.0 * jax.random.uniform(keys[6], (MHEADS,), jnp.float32) ** level_of(keys[6], (MHEADS,), ((0, 4),), -0.2, 0.2), 0.5, 1.5),
        "norm_gain": jnp.clip(1.0 + 0.15 * jax.random.normal(keys[7], (MHEADS * HEAD_P,), jnp.float32), 0.25, 1.75),
        "doc_lengths": uneven_parts(own_keys[8], NDOCS, TOKENS, DOC_MAX, 2).astype(jnp.int32),
        "queries": draw_queries(jax.random.fold_in(jax.random.fold_in(keys[12], part), 71), part),
        "keys_in": draw_keys_in(jax.random.fold_in(jax.random.fold_in(keys[12], part), 71), part),
        "values_in": normal_values(own_keys[11], (TOKENS, KVHEADS * HEAD_D), 1.0, 6.0, ((0, 8), (1, 2))),
    }


def narrowed(values):
    return lax.optimization_barrier(values.astype(jnp.bfloat16)).astype(jnp.float32)

def doc_starts(doc_lengths):
    return (jnp.cumsum(doc_lengths) - doc_lengths).astype(jnp.int32)

def segment_of(starts, positions):
    return lax.optimization_barrier(jnp.sum((starts[None, :] <= positions[:, None]).astype(jnp.int32), axis=1)) - 1

def mamba_reference(ssm_input, ssm_gate, input_map, output_map, step_size, decay_log, skip_gain, norm_gain, starts):
    block_rows = TOK_DEV * N_HEAD
    block_count = TOKENS // block_rows
    group_count = N_HEAD * N_TP
    per_group = MHEADS // group_count
    rates = -jnp.exp(decay_log)

    def block_step(carried, block_index):
        first_row = (block_index * block_rows).astype(jnp.int32)
        positions = first_row + jnp.arange(block_rows, dtype=jnp.int32)
        segment_ids = segment_of(starts, positions)
        segment_before = jnp.sum((starts <= first_row - 1).astype(jnp.int32)) - 1
        inputs_f = lax.dynamic_slice_in_dim(ssm_input, first_row, block_rows, 0).astype(jnp.float32)
        inputs_f = inputs_f.reshape(block_rows, MHEADS, HEAD_P)
        steps_here = lax.dynamic_slice_in_dim(step_size, first_row, block_rows, 1)
        cumulative = jnp.cumsum(steps_here * rates[:, None], axis=1)
        in_maps = lax.dynamic_slice_in_dim(input_map, first_row, block_rows, 0).astype(jnp.float32)
        in_maps = in_maps.reshape(block_rows, group_count, STATE)
        out_maps = lax.dynamic_slice_in_dim(output_map, first_row, block_rows, 0).astype(jnp.float32)
        out_maps = out_maps.reshape(block_rows, group_count, STATE)
        intersection = jnp.einsum('tgn,sgn->gts', out_maps, in_maps)
        intersection = jnp.repeat(intersection, per_group, axis=0)
        same_doc = (segment_ids[:, None] == segment_ids[None, :]) & (positions[:, None] >= positions[None, :])
        differences = cumulative[:, :, None] - cumulative[:, None, :]
        weights = jnp.where(same_doc[None], jnp.exp(jnp.where(same_doc[None], differences, 0.0)) * intersection * steps_here[:, None, :], 0.0)
        intra = jnp.einsum('hts,shp->thp', narrowed(weights), inputs_f)
        tail_weights = jnp.where((segment_ids == segment_ids[-1])[None, :], jnp.exp(cumulative[:, -1:] - cumulative) * steps_here, 0.0)
        scaled_input = narrowed(jnp.transpose(tail_weights)[:, :, None] * inputs_f)
        local_state = jnp.einsum('sgn,sghp->ghnp', in_maps, scaled_input.reshape(block_rows, group_count, per_group, HEAD_P))
        local_state = local_state.reshape(MHEADS, STATE, HEAD_P)
        inbound = narrowed(carried)
        inter = jnp.einsum('tgn,ghnp->tghp', out_maps, inbound.reshape(group_count, per_group, STATE, HEAD_P))
        inter = inter.reshape(block_rows, MHEADS, HEAD_P)
        reach_scale = jnp.where((segment_ids == segment_before)[None, :], jnp.exp(cumulative), 0.0)
        inter = inter * jnp.transpose(reach_scale)[:, :, None]
        combined = intra + inter + skip_gain[None, :, None] * inputs_f
        gates = lax.dynamic_slice_in_dim(ssm_gate, first_row, block_rows, 0).astype(jnp.float32)
        gates = gates.reshape(block_rows, group_count, per_group * HEAD_P)
        gated = combined.reshape(block_rows, group_count, per_group * HEAD_P) * jax.nn.silu(gates)
        normed = gated * lax.rsqrt(lax.optimization_barrier(jnp.mean(gated * gated, axis=2, keepdims=True)) + 1e-05)
        result = (normed.reshape(block_rows, MHEADS * HEAD_P) * norm_gain[None, :]).astype(jnp.bfloat16)
        any_start = jnp.any((starts >= first_row) & (starts < first_row + block_rows))
        factor = jnp.where(any_start, 0.0, jnp.exp(cumulative[:, -1]))
        return (local_state + factor[:, None, None] * carried, result)
    initial = jnp.zeros((MHEADS, STATE, HEAD_P), jnp.float32)
    finished, results = lax.scan(block_step, initial, jnp.arange(block_count, dtype=jnp.int32))
    return results.reshape(TOKENS, MHEADS * HEAD_P)

def attention_reference(queries, keys_in, values_in, starts):
    block_rows = TOK_DEV * N_HEAD
    block_count = TOKENS // block_rows
    span_rows = (REACH + 1) * block_rows
    group_size = QHEADS // KVHEADS
    padding = jnp.zeros((REACH * block_rows, KVHEADS * HEAD_D), jnp.bfloat16)
    keys_padded = jnp.concatenate([padding, keys_in], axis=0)
    values_padded = jnp.concatenate([padding, values_in], axis=0)

    def one_block(block_index):
        first_row = (block_index * block_rows).astype(jnp.int32)
        query_block = lax.dynamic_slice_in_dim(queries, first_row, block_rows, 0).astype(jnp.float32)
        query_block = query_block.reshape(block_rows, KVHEADS, group_size, HEAD_D)
        key_block = lax.dynamic_slice_in_dim(keys_padded, first_row, span_rows, 0).astype(jnp.float32)
        key_block = key_block.reshape(span_rows, KVHEADS, HEAD_D)
        value_block = lax.dynamic_slice_in_dim(values_padded, first_row, span_rows, 0).astype(jnp.float32)
        value_block = value_block.reshape(span_rows, KVHEADS, HEAD_D)
        query_pos = first_row + jnp.arange(block_rows, dtype=jnp.int32)
        key_pos = first_row - REACH * block_rows + jnp.arange(span_rows, dtype=jnp.int32)
        allowed = segment_of(starts, query_pos)[:, None] == segment_of(starts, key_pos)[None, :]
        allowed = allowed & (key_pos[None, :] <= query_pos[:, None]) & (key_pos[None, :] >= 0)
        logits = jnp.einsum('tkgd,skd->kgts', query_block, key_block) * (1.0 / math.sqrt(HEAD_D))
        masked = jnp.where(allowed, logits, -jnp.inf)
        highest = lax.optimization_barrier(jnp.max(masked, axis=3, keepdims=True))
        probs = jnp.where(allowed, jnp.exp(masked - highest), 0.0)
        denominator = lax.optimization_barrier(jnp.sum(probs, axis=3))
        mixed = jnp.einsum('kgts,skd->tkgd', narrowed(probs), value_block)
        mixed = mixed / jnp.transpose(denominator, (2, 0, 1))[:, :, :, None]
        return mixed.reshape(block_rows, QHEADS * HEAD_D).astype(jnp.bfloat16)
    results = lax.map(one_block, jnp.arange(block_count, dtype=jnp.int32))
    return results.reshape(TOKENS, QHEADS * HEAD_D)

def reference(ssm_input, ssm_gate, input_map, output_map, step_size, decay_log, skip_gain, norm_gain, doc_lengths, queries, keys_in, values_in):
    starts = doc_starts(doc_lengths)
    ssm_out = mamba_reference(ssm_input, ssm_gate, input_map, output_map, step_size, decay_log, skip_gain, norm_gain, starts)
    attn_out = attention_reference(queries, keys_in, values_in, starts)
    return (ssm_out, attn_out)
```

```python
import functools
import math

import jax
import jax.numpy as jnp
from jax import lax
from jax.experimental import pallas as pl
from jax.experimental.pallas import tpu as pltpu
from jax.sharding import PartitionSpec as P

HEAD_P = 64
HEAD_D = 128
REACH = 2
MESH = pl.DeviceIdType.MESH
TILE = 256
F32 = jnp.float32
BF16 = jnp.bfloat16


def dot(a, b):
    return jnp.dot(a, b, preferred_element_type=F32)


def dot_nt(a, b):
    return lax.dot_general(a, b, (((1,), (1,)), ((), ())), preferred_element_type=F32)


def split3(v):
    hi = v.astype(BF16).astype(F32)
    mid = (v - hi).astype(BF16).astype(F32)
    lo = (v - hi - mid).astype(BF16).astype(F32)
    return hi, mid, lo


def column(row, count):
    r = lax.broadcasted_iota(jnp.int32, (count, count), 0)
    c = lax.broadcasted_iota(jnp.int32, (count, count), 1)
    return jnp.sum(jnp.where(r == c, row, 0.0), axis=1, keepdims=True)


def stacked(v):
    hi, mid, lo = split3(v)
    return jnp.concatenate([hi, mid, lo, jnp.zeros_like(v)], axis=0).T.astype(BF16)


def kernel(
    nz, nh, width,
    dl_ref, x_ref, z_ref, b_ref, c_ref, step_ref, decay_ref, skip_ref, norm_ref, q_ref, k_ref, v_ref,
    so_ref, ao_ref,
    kv, s_in, s_out, local, pre, spread, e_parts, g_parts, row_parts, m_ref, bm_ref, cm_ref, rows_ref, bias_ref,
    kv_recv, z_send, x_send, s_recv, s_send,
):
    z = lax.axis_index("seq")
    x = lax.axis_index("head")
    rows, cols = x_ref.shape
    heads = step_ref.shape[0]
    nt = rows // TILE
    chunks = cols // width
    tok = q_ref.shape[0]
    kvw = k_ref.shape[1]
    slots = REACH * nh + 1
    own = slots - 1
    docs = dl_ref.shape[0]
    position = z * nh + x
    first = z * rows

    barrier = pltpu.get_barrier_semaphore()
    has_prev, has_next = z > 0, z < nz - 1

    def greet(axis, index):
        pl.semaphore_signal(barrier, inc=1, device_id={axis: index}, device_id_type=MESH)

    kv[own, :, :kvw] = k_ref[...]
    kv[own, :, kvw:] = v_ref[...]

    @pl.when(has_prev)
    def _():
        greet("seq", z - 1)

    @pl.when(has_next)
    def _():
        greet("seq", z + 1)

    for d in range(1, nh):
        greet("head", lax.rem(x + d, nh))

    pl.semaphore_wait(barrier, has_prev.astype(jnp.int32) + has_next.astype(jnp.int32) + nh - 1)

    def to_next(source, target, sem):
        return pltpu.make_async_remote_copy(
            src_ref=kv.at[source], dst_ref=kv.at[target], send_sem=z_send.at[sem], recv_sem=kv_recv.at[target],
            device_id={"seq": z + 1}, device_id_type=MESH)

    def to_side(source, target, sem, peer):
        return pltpu.make_async_remote_copy(
            src_ref=kv.at[source], dst_ref=kv.at[target], send_sem=x_send.at[sem], recv_sem=kv_recv.at[target],
            device_id={"head": peer}, device_id_type=MESH)

    def side_copies(d):
        up, down = x + d < nh, x - d >= 0
        base = (d - 1) * 4
        return {
            0: [(up, lambda: to_side(own, own - d, base, x + d))],
            1: [
                (up & has_prev, lambda: to_side(nh, nh - d, base + 1, x + d)),
                (down & has_prev, lambda: to_side(nh, nh + d, base + 2, x - d)),
            ],
            2: [(down & (z > 1), lambda: to_side(0, d, base + 3, x - d))],
        }

    def start_stage(stage):
        for d in range(1, nh):
            for exists, make in side_copies(d)[stage]:
                pl.when(exists)(lambda make=make: make().start())

    def arrived(slot):
        pltpu.make_async_copy(kv.at[slot], kv.at[slot], kv_recv.at[slot]).wait()

    pl.when(has_next)(lambda: to_next(own, nh, 0).start())
    start_stage(0)

    for slot in range(own):
        @pl.when(position - own + slot < 0)
        def _():
            kv[slot] = jnp.zeros((tok, 2 * kvw), BF16)

    @pl.when(z == 0)
    def _():
        s_in[...] = jnp.zeros_like(s_in)

    def doc_start(pos):
        best = jnp.zeros_like(pos)
        start = jnp.int32(0)
        for d in range(docs):
            best = jnp.where(start <= pos, jnp.maximum(best, start), best)
            start = start + dl_ref[d]
        return best

    end_start = doc_start(first + rows - 1)
    rates = column(-jnp.exp(decay_ref[...]), heads)
    step = step_ref[...]
    s_iota = lax.broadcasted_iota(jnp.int32, (rows, rows), 0)
    t_iota = lax.broadcasted_iota(jnp.int32, (rows, rows), 1)
    upper = jnp.where(s_iota <= t_iota, 1.0, 0.0).astype(BF16)
    hi, mid, lo = split3(step * rates)
    cum = dot(hi.astype(BF16), upper) + dot(mid.astype(BF16), upper) + dot(lo.astype(BF16), upper)
    last = cum[:, rows - 1 : rows]
    factor = jnp.where(end_start >= first, 0.0, jnp.exp(last))
    lane = lax.broadcasted_iota(jnp.int32, (heads, 128), 1)
    table = jnp.where(lane == 0, factor, jnp.where(lane == 1, column(skip_ref[...], heads), 0.0))
    pair = 0
    for i in range(nt):
        mark = i * TILE + TILE // 2 - 1
        ref = cum[:, mark : mark + 1]
        table = jnp.where(lane == 2 + 2 * i, jnp.exp(ref), table)
        table = jnp.where(lane == 3 + 2 * i, jnp.exp(last - ref), table)
        here = slice(i * TILE, (i + 1) * TILE)
        e_parts[here, :] = stacked(jnp.exp(cum[:, here] - ref))
        for j in range(i + 1):
            there = slice(j * TILE, (j + 1) * TILE)
            g_parts[pair] = stacked(jnp.exp(ref - cum[:, there]) * step[:, there])
            pair += 1
    row_parts[...] = stacked(table)[:16]
    r_iota = lax.broadcasted_iota(jnp.int32, spread.shape, 0)
    h_iota = lax.broadcasted_iota(jnp.int32, spread.shape, 1) // HEAD_P
    hit = r_iota == h_iota
    for piece in range(1, 4):
        hit = hit | (r_iota == h_iota + piece * heads)
    spread[...] = jnp.where(hit, 1.0, 0.0).astype(BF16)
    rows_ref[...] = dot(row_parts[...], spread[...])

    pos_t = first + lax.broadcasted_iota(jnp.int32, (rows, 1), 0)
    start_t = doc_start(pos_t)
    pos_s = first + lax.broadcasted_iota(jnp.int32, (rows, rows), 1)
    inter = dot_nt(c_ref[...], b_ref[...])
    m_ref[...] = jnp.where((pos_s >= start_t) & (pos_s <= pos_t), inter, 0.0).astype(BF16)
    bm_ref[...] = jnp.where(pos_t >= end_start, b_ref[...].astype(F32), 0.0).T.astype(BF16)
    cm_ref[...] = jnp.where(start_t < first, c_ref[...].astype(F32), 0.0).astype(BF16)
    query_t = position * tok + lax.broadcasted_iota(jnp.int32, (tok, 1), 0)
    key_s = (position - own) * tok + lax.broadcasted_iota(jnp.int32, (tok, slots * tok), 1)
    bias_ref[...] = jnp.where((key_s >= doc_start(query_t)) & (key_s <= query_t), 0.0, -jnp.inf)

    def state_copy(c):
        return pltpu.make_async_remote_copy(
            src_ref=s_out.at[c], dst_ref=s_in.at[c], send_sem=s_send.at[c], recv_sem=s_recv.at[c],
            device_id={"seq": z + 1}, device_id_type=MESH)

    def chunk_of(c):
        return pl.ds(pl.multiple_of(c * width, width), width)

    def block_part(c, _):
        at = chunk_of(c)
        state = jnp.zeros((bm_ref.shape[0], width), F32)
        pair = 0
        for i in range(nt):
            here = slice(i * TILE, (i + 1) * TILE)
            total = jnp.zeros((TILE, width), F32)
            for j in range(i + 1):
                there = slice(j * TILE, (j + 1) * TILE)
                scaled = (dot(g_parts[pair], spread[:, at]) * x_ref[there, at].astype(F32)).astype(BF16)
                total += dot(m_ref[here, there], scaled)
                pair += 1
            pre[here, at] = total
            state += dot(bm_ref[:, here], scaled) * rows_ref[3 + 2 * i : 4 + 2 * i, at]
        local[c] = state

        @pl.when(z == 0)
        def _():
            s_out[c] = state.astype(BF16)
            if nz > 1:
                state_copy(c).start()
        return 0

    lax.fori_loop(0, chunks, block_part, 0)

    @pl.when(has_prev)
    def _():
        arrived(nh)
        pl.when(has_next)(lambda: to_next(nh, 0, 1).start())

    start_stage(1)
    pl.when(z > 1)(lambda: arrived(0))
    start_stage(2)

    def state_part(c, squares):
        at = chunk_of(c)

        @pl.when(has_prev)
        def _():
            pltpu.make_async_copy(s_in.at[c], s_in.at[c], s_recv.at[c]).wait()

            @pl.when(has_next)
            def _():
                s_out[c] = (local[c] + rows_ref[0:1, at] * s_in[c].astype(F32)).astype(BF16)
                state_copy(c).start()

        inbound = s_in[c].astype(F32)
        sums = []
        for i in range(nt):
            here = slice(i * TILE, (i + 1) * TILE)
            scaled = (inbound * rows_ref[2 + 2 * i : 3 + 2 * i, at]).astype(BF16)
            total = (pre[here, at] + dot(cm_ref[here, :], scaled)) * dot(e_parts[here, :], spread[:, at])
            total += rows_ref[1:2, at] * x_ref[here, at].astype(F32)
            gate = z_ref[here, at].astype(F32)
            gated = total * (gate / (1.0 + jnp.exp(-gate)))
            pre[here, at] = gated
            sums.append(jnp.sum(gated * gated, axis=1, keepdims=True))
        return squares + jnp.concatenate(sums, axis=0)

    squares = lax.fori_loop(0, chunks, state_part, jnp.zeros((rows, 1), F32))
    inverse = lax.rsqrt(squares * (1.0 / cols) + 1e-05)

    def norm_part(c, _):
        at = chunk_of(c)
        so_ref[:, at] = (pre[:, at] * inverse * norm_ref[:, at]).astype(BF16)
        return 0

    lax.fori_loop(0, chunks, norm_part, 0)

    for slot in range(own):
        if slot not in (0, nh):
            pl.when(position - own + slot >= 0)(lambda slot=slot: arrived(slot))
    kv_heads = kvw // HEAD_D
    group = q_ref.shape[1] // kvw
    scale = 1.0 / math.sqrt(HEAD_D)

    def attend(g, _):
        def at(start):
            return pl.ds(pl.multiple_of(start, HEAD_D), HEAD_D)

        query = jnp.concatenate([q_ref[:, at((g * group + j) * HEAD_D)] for j in range(group)], axis=0)
        key = jnp.concatenate([kv[s, :, at(g * HEAD_D)] for s in range(slots)], axis=0)
        value = jnp.concatenate([kv[s, :, at(kvw + g * HEAD_D)] for s in range(slots)], axis=0)
        bias = jnp.concatenate([bias_ref[...]] * group, axis=0)
        logits = dot_nt(query, key) * scale + bias
        probs = jnp.exp(logits - jnp.max(logits, axis=1, keepdims=True))
        mixed = dot(probs.astype(BF16), value) / jnp.sum(probs, axis=1, keepdims=True)
        for j in range(group):
            ao_ref[:, at((g * group + j) * HEAD_D)] = mixed[j * tok : (j + 1) * tok].astype(BF16)
        return 0

    lax.fori_loop(0, kv_heads, attend, 0)

    @pl.when(has_next)
    def _():
        to_next(own, nh, 0).wait_send()
        pl.when(has_prev)(lambda: to_next(nh, 0, 1).wait_send())

        def sent(c, _):
            state_copy(c).wait_send()
            return 0

        lax.fori_loop(0, chunks, sent, 0)

    for d in range(1, nh):
        for copies in side_copies(d).values():
            for exists, make in copies:
                pl.when(exists)(lambda make=make: make().wait_send())


def on_device(
    nz, nh,
    ssm_input, ssm_gate, input_map, output_map, step_size, decay_log, skip_gain, norm_gain, doc_lengths,
    queries, keys_in, values_in,
):
    rows, cols = ssm_input.shape
    heads = step_size.shape[0]
    state = input_map.shape[1]
    tok, kvw = keys_in.shape
    width = min(512, cols)
    chunks = cols // width
    nt = rows // TILE
    slots = REACH * nh + 1
    vmem = pl.BlockSpec(memory_space=pltpu.VMEM)
    dma = pltpu.SemaphoreType.DMA
    return pl.pallas_call(
        functools.partial(kernel, nz, nh, width),
        out_shape=(
            jax.ShapeDtypeStruct((rows, cols), BF16),
            jax.ShapeDtypeStruct(queries.shape, BF16),
        ),
        in_specs=[pl.BlockSpec(memory_space=pltpu.SMEM)] + [vmem] * 11,
        out_specs=(vmem, vmem),
        scratch_shapes=[
            pltpu.VMEM((slots, tok, 2 * kvw), BF16),
            pltpu.VMEM((chunks, state, width), BF16),
            pltpu.VMEM((chunks, state, width), BF16),
            pltpu.VMEM((chunks, state, width), F32),
            pltpu.VMEM((rows, cols), F32),
            pltpu.VMEM((4 * heads, cols), BF16),
            pltpu.VMEM((rows, 4 * heads), BF16),
            pltpu.VMEM((nt * (nt + 1) // 2, TILE, 4 * heads), BF16),
            pltpu.VMEM((16, 4 * heads), BF16),
            pltpu.VMEM((rows, rows), BF16),
            pltpu.VMEM((state, rows), BF16),
            pltpu.VMEM((rows, state), BF16),
            pltpu.VMEM((16, cols), F32),
            pltpu.VMEM((tok, slots * tok), F32),
            dma((slots,)),
            dma((2,)),
            dma((max(1, 4 * (nh - 1)),)),
            dma((chunks,)),
            dma((chunks,)),
        ],
        compiler_params=pltpu.CompilerParams(
            collective_id=0, has_side_effects=True, vmem_limit_bytes=48 * 1024 * 1024
        ),
    )(
        doc_lengths, ssm_input, ssm_gate, input_map, output_map, step_size, decay_log[None, :], skip_gain[None, :],
        norm_gain[None, :], queries, keys_in, values_in,
    )


def solution(mesh):
    channels = P(("groups", "seq"), ("head", "tp"))
    per_head = P(("head", "tp"))
    positions = P(("groups", "seq", "head"), "tp")
    return jax.shard_map(
        functools.partial(on_device, mesh.shape["seq"], mesh.shape["head"]),
        mesh=mesh,
        in_specs=(
            channels, channels, channels, channels, P(("head", "tp"), ("groups", "seq")), per_head, per_head, per_head,
            P("groups"), positions, positions, positions,
        ),
        out_specs=(channels, positions),
        check_vma=False,
    )
```

```python
import functools
import math

import jax
import jax.numpy as jnp
from jax import lax
from jax.experimental import pallas as pl
from jax.experimental.pallas import tpu as pltpu
from jax.sharding import PartitionSpec as P

HEAD_P = 64
HEAD_D = 128
REACH = 2
MESH = pl.DeviceIdType.MESH
TILE = 256
F32 = jnp.float32
BF16 = jnp.bfloat16


def dot(a, b):
    return jnp.dot(a, b, preferred_element_type=F32)


def dot_nt(a, b):
    return lax.dot_general(a, b, (((1,), (1,)), ((), ())), preferred_element_type=F32)


def split3(v):
    hi = v.astype(BF16).astype(F32)
    mid = (v - hi).astype(BF16).astype(F32)
    lo = (v - hi - mid).astype(BF16).astype(F32)
    return hi, mid, lo


def column(row, count):
    r = lax.broadcasted_iota(jnp.int32, (count, count), 0)
    c = lax.broadcasted_iota(jnp.int32, (count, count), 1)
    return jnp.sum(jnp.where(r == c, row, 0.0), axis=1, keepdims=True)


def stacked(v):
    hi, mid, lo = split3(v)
    return jnp.concatenate([hi, mid, lo, jnp.zeros_like(v)], axis=0).T.astype(BF16)


def kernel(
    nz, nh, width,
    dl_hbm, x_hbm, z_hbm, b_hbm, c_hbm, step_hbm, decay_hbm, skip_hbm, norm_hbm, q_hbm, k_hbm, v_hbm,
    so_ref, ao_ref,
    dl_ref, x_ref, z_ref, b_ref, c_ref, step_ref, decay_ref, skip_ref, norm_ref, q_ref,
    kv, s_in, s_out, local, pre, spread, e_parts, g_parts, row_parts, m_ref, bm_ref, cm_ref, rows_ref, bias_ref,
    mixed_ref, top_ref, sum_ref,
    loads, kv_recv, z_send, x_send, s_recv, s_send,
):
    z = lax.axis_index("seq")
    x = lax.axis_index("head")
    rows, cols = x_ref.shape
    heads = step_ref.shape[0]
    nt = rows // TILE
    chunks = cols // width
    tok = q_ref.shape[0]
    kvw = k_hbm.shape[1]
    slots = REACH * nh + 1
    own = slots - 1
    docs = dl_ref.shape[0]
    position = z * nh + x
    first = z * rows

    barrier = pltpu.get_barrier_semaphore()
    has_prev, has_next = z > 0, z < nz - 1

    def greet(axis, index):
        pl.semaphore_signal(barrier, inc=1, device_id={axis: index}, device_id_type=MESH)

    moves = [
        (k_hbm, kv.at[own, :, pl.ds(0, kvw)]), (v_hbm, kv.at[own, :, pl.ds(kvw, kvw)]), (step_hbm, step_ref),
        (decay_hbm, decay_ref), (skip_hbm, skip_ref), (dl_hbm, dl_ref), (b_hbm, b_ref), (c_hbm, c_ref), (x_hbm, x_ref),
        (q_hbm, q_ref), (z_hbm, z_ref), (norm_hbm, norm_ref),
    ]
    moves = [pltpu.make_async_copy(source, target, loads.at[i]) for i, (source, target) in enumerate(moves)]
    for move in moves:
        move.start()

    @pl.when(has_prev)
    def _():
        greet("seq", z - 1)

    @pl.when(has_next)
    def _():
        greet("seq", z + 1)

    for d in range(1, nh):
        greet("head", lax.rem(x + d, nh))

    pl.semaphore_wait(barrier, has_prev.astype(jnp.int32) + has_next.astype(jnp.int32) + nh - 1)

    moves[0].wait()
    moves[1].wait()

    def to_next(source, target, sem):
        return pltpu.make_async_remote_copy(
            src_ref=kv.at[source], dst_ref=kv.at[target], send_sem=z_send.at[sem], recv_sem=kv_recv.at[target],
            device_id={"seq": z + 1}, device_id_type=MESH)

    def to_side(source, target, sem, peer):
        return pltpu.make_async_remote_copy(
            src_ref=kv.at[source], dst_ref=kv.at[target], send_sem=x_send.at[sem], recv_sem=kv_recv.at[target],
            device_id={"head": peer}, device_id_type=MESH)

    def side_copies(d):
        up, down = x + d < nh, x - d >= 0
        base = (d - 1) * 4
        return {
            0: [(up, lambda: to_side(own, own - d, base, x + d))],
            1: [
                (up & has_prev, lambda: to_side(nh, nh - d, base + 1, x + d)),
                (down & has_prev, lambda: to_side(nh, nh + d, base + 2, x - d)),
            ],
            2: [(down & (z > 1), lambda: to_side(0, d, base + 3, x - d))],
        }

    def start_stage(stage):
        for d in range(1, nh):
            for exists, make in side_copies(d)[stage]:
                pl.when(exists)(lambda make=make: make().start())

    def arrived(slot):
        pltpu.make_async_copy(kv.at[slot], kv.at[slot], kv_recv.at[slot]).wait()

    pl.when(has_next)(lambda: to_next(own, nh, 0).start())
    start_stage(0)

    for slot in range(own):
        @pl.when(position - own + slot < 0)
        def _():
            kv[slot] = jnp.zeros((tok, 2 * kvw), BF16)

    @pl.when(z == 0)
    def _():
        s_in[...] = jnp.zeros_like(s_in)

    for move in moves[2:8]:
        move.wait()

    def doc_start(pos):
        best = jnp.zeros_like(pos)
        start = jnp.int32(0)
        for d in range(docs):
            best = jnp.where(start <= pos, jnp.maximum(best, start), best)
            start = start + dl_ref[d]
        return best

    end_start = doc_start(first + rows - 1)
    rates = column(-jnp.exp(decay_ref[...]), heads)
    step = step_ref[...]
    s_iota = lax.broadcasted_iota(jnp.int32, (rows, rows), 0)
    t_iota = lax.broadcasted_iota(jnp.int32, (rows, rows), 1)
    upper = jnp.where(s_iota <= t_iota, 1.0, 0.0).astype(BF16)
    hi, mid, lo = split3(step * rates)
    cum = dot(hi.astype(BF16), upper) + dot(mid.astype(BF16), upper) + dot(lo.astype(BF16), upper)
    last = cum[:, rows - 1 : rows]
    factor = jnp.where(end_start >= first, 0.0, jnp.exp(last))
    lane = lax.broadcasted_iota(jnp.int32, (heads, 128), 1)
    table = jnp.where(lane == 0, factor, jnp.where(lane == 1, column(skip_ref[...], heads), 0.0))
    pair = 0
    for i in range(nt):
        mark = i * TILE + TILE // 2 - 1
        ref = cum[:, mark : mark + 1]
        table = jnp.where(lane == 2 + 2 * i, jnp.exp(ref), table)
        table = jnp.where(lane == 3 + 2 * i, jnp.exp(last - ref), table)
        here = slice(i * TILE, (i + 1) * TILE)
        e_parts[here, :] = stacked(jnp.exp(cum[:, here] - ref))
        for j in range(i + 1):
            there = slice(j * TILE, (j + 1) * TILE)
            g_parts[pair] = stacked(jnp.exp(ref - cum[:, there]) * step[:, there])
            pair += 1
    row_parts[...] = stacked(table)[:16]
    r_iota = lax.broadcasted_iota(jnp.int32, spread.shape, 0)
    h_iota = lax.broadcasted_iota(jnp.int32, spread.shape, 1) // HEAD_P
    hit = r_iota == h_iota
    for piece in range(1, 4):
        hit = hit | (r_iota == h_iota + piece * heads)
    spread[...] = jnp.where(hit, 1.0, 0.0).astype(BF16)
    rows_ref[...] = dot(row_parts[...], spread[...])

    pos_t = first + lax.broadcasted_iota(jnp.int32, (rows, 1), 0)
    start_t = doc_start(pos_t)
    pos_s = first + lax.broadcasted_iota(jnp.int32, (rows, rows), 1)
    inter = dot_nt(c_ref[...], b_ref[...])
    m_ref[...] = jnp.where((pos_s >= start_t) & (pos_s <= pos_t), inter, 0.0).astype(BF16)
    bm_ref[...] = jnp.where(pos_t >= end_start, b_ref[...].astype(F32), 0.0).T.astype(BF16)
    cm_ref[...] = jnp.where(start_t < first, c_ref[...].astype(F32), 0.0).astype(BF16)
    query_t = position * tok + lax.broadcasted_iota(jnp.int32, (tok, 1), 0)
    key_s = (position - own) * tok + lax.broadcasted_iota(jnp.int32, (tok, slots * tok), 1)
    bias_ref[...] = jnp.where((key_s >= doc_start(query_t)) & (key_s <= query_t), 0.0, -jnp.inf)

    def state_copy(c):
        return pltpu.make_async_remote_copy(
            src_ref=s_out.at[c], dst_ref=s_in.at[c], send_sem=s_send.at[c], recv_sem=s_recv.at[c],
            device_id={"seq": z + 1}, device_id_type=MESH)

    def chunk_of(c):
        return pl.ds(pl.multiple_of(c * width, width), width)

    def block_part(c, _):
        at = chunk_of(c)
        state = jnp.zeros((bm_ref.shape[0], width), F32)
        pair = 0
        for i in range(nt):
            here = slice(i * TILE, (i + 1) * TILE)
            total = jnp.zeros((TILE, width), F32)
            for j in range(i + 1):
                there = slice(j * TILE, (j + 1) * TILE)
                scaled = (dot(g_parts[pair], spread[:, at]) * x_ref[there, at].astype(F32)).astype(BF16)
                total += dot(m_ref[here, there], scaled)
                pair += 1
            pre[here, at] = total
            state += dot(bm_ref[:, here], scaled) * rows_ref[3 + 2 * i : 4 + 2 * i, at]
        local[c] = state

        @pl.when(z == 0)
        def _():
            s_out[c] = state.astype(BF16)
            if nz > 1:
                state_copy(c).start()
        return 0

    moves[8].wait()
    lax.fori_loop(0, chunks, block_part, 0)
    for move in moves[9:]:
        move.wait()

    @pl.when(has_prev)
    def _():
        arrived(nh)
        pl.when(has_next)(lambda: to_next(nh, 0, 1).start())

    start_stage(1)
    kv_heads = kvw // HEAD_D
    group = q_hbm.shape[1] // kvw
    scale = 1.0 / math.sqrt(HEAD_D)

    def head_at(start):
        return pl.ds(pl.multiple_of(start, HEAD_D), HEAD_D)

    def logits_of(g, low, high):
        query = jnp.concatenate([q_ref[:, head_at((g * group + j) * HEAD_D)] for j in range(group)], axis=0)
        key = jnp.concatenate([kv[s, :, head_at(g * HEAD_D)] for s in range(low, high)], axis=0)
        value = jnp.concatenate([kv[s, :, head_at(kvw + g * HEAD_D)] for s in range(low, high)], axis=0)
        bias = jnp.concatenate([bias_ref[:, low * tok : high * tok]] * group, axis=0)
        return dot_nt(query, key) * scale + bias, value

    def near(g):
        logits, value = logits_of(g, nh, slots)
        top = jnp.max(logits, axis=1, keepdims=True)
        probs = jnp.exp(logits - top)
        mixed_ref[g] = dot(probs.astype(BF16), value)
        top_ref[g] = top
        sum_ref[g] = jnp.sum(probs, axis=1, keepdims=True)

    def far(g, _):
        logits, value = logits_of(g, 0, nh)
        before = top_ref[g]
        top = jnp.maximum(before, jnp.max(logits, axis=1, keepdims=True))
        probs = jnp.exp(logits - top)
        keep = jnp.exp(before - top)
        total = jnp.sum(probs, axis=1, keepdims=True) + sum_ref[g] * keep
        mixed = (dot(probs.astype(BF16), value) + mixed_ref[g] * keep) / total
        for j in range(group):
            ao_ref[:, head_at((g * group + j) * HEAD_D)] = mixed[j * tok : (j + 1) * tok].astype(BF16)
        return 0

    def far_all():
        for slot in range(1, nh):
            pl.when(position - own + slot >= 0)(lambda slot=slot: arrived(slot))
        lax.fori_loop(0, kv_heads, far, 0)

    def state_part(c, squares):
        at = chunk_of(c)

        @pl.when(has_prev)
        def _():
            pltpu.make_async_copy(s_in.at[c], s_in.at[c], s_recv.at[c]).wait()

            @pl.when(has_next)
            def _():
                s_out[c] = (local[c] + rows_ref[0:1, at] * s_in[c].astype(F32)).astype(BF16)
                state_copy(c).start()

        inbound = s_in[c].astype(F32)
        sums = []
        for i in range(nt):
            here = slice(i * TILE, (i + 1) * TILE)
            scaled = (inbound * rows_ref[2 + 2 * i : 3 + 2 * i, at]).astype(BF16)
            total = (pre[here, at] + dot(cm_ref[here, :], scaled)) * dot(e_parts[here, :], spread[:, at])
            total += rows_ref[1:2, at] * x_ref[here, at].astype(F32)
            gate = z_ref[here, at].astype(F32)
            gated = total * (gate / (1.0 + jnp.exp(-gate)))
            pre[here, at] = gated
            sums.append(jnp.sum(gated * gated, axis=1, keepdims=True))
        return squares + jnp.concatenate(sums, axis=0)

    def near_part(g, _):
        near(g)
        return 0

    def mixed_part(c, squares):
        squares = state_part(c, squares)

        @pl.when(c == 0)
        def _():
            for slot in range(nh + 1, own):
                pl.when(position - own + slot >= 0)(lambda slot=slot: arrived(slot))

        pl.when(c < kv_heads)(lambda: near(c))
        return squares

    squares = mixed_part(0, jnp.zeros((rows, 1), F32))
    pl.when(z > 1)(lambda: arrived(0))
    start_stage(2)
    squares = lax.fori_loop(1, chunks - 1, mixed_part, squares)
    lax.fori_loop(chunks - 1, kv_heads, near_part, 0)
    pl.when(z == nz - 1)(far_all)
    squares = state_part(chunks - 1, squares)
    inverse = lax.rsqrt(squares * (1.0 / cols) + 1e-05)

    def norm_part(c, _):
        at = chunk_of(c)
        so_ref[:, at] = (pre[:, at] * inverse * norm_ref[:, at]).astype(BF16)
        return 0

    lax.fori_loop(0, chunks, norm_part, 0)
    pl.when(z < nz - 1)(far_all)

    @pl.when(has_next)
    def _():
        to_next(own, nh, 0).wait_send()
        pl.when(has_prev)(lambda: to_next(nh, 0, 1).wait_send())

        def sent(c, _):
            state_copy(c).wait_send()
            return 0

        lax.fori_loop(0, chunks, sent, 0)

    for d in range(1, nh):
        for copies in side_copies(d).values():
            for exists, make in copies:
                pl.when(exists)(lambda make=make: make().wait_send())


def on_device(
    nz, nh,
    ssm_input, ssm_gate, input_map, output_map, step_size, decay_log, skip_gain, norm_gain, doc_lengths,
    queries, keys_in, values_in,
):
    rows, cols = ssm_input.shape
    heads = step_size.shape[0]
    state = input_map.shape[1]
    tok, kvw = keys_in.shape
    width = min(512, cols)
    chunks = cols // width
    nt = rows // TILE
    slots = REACH * nh + 1
    vmem = pl.BlockSpec(memory_space=pltpu.VMEM)
    dma = pltpu.SemaphoreType.DMA
    return pl.pallas_call(
        functools.partial(kernel, nz, nh, width),
        out_shape=(
            jax.ShapeDtypeStruct((rows, cols), BF16),
            jax.ShapeDtypeStruct(queries.shape, BF16),
        ),
        in_specs=[pl.BlockSpec(memory_space=pltpu.HBM)] * 12,
        out_specs=(vmem, vmem),
        scratch_shapes=[
            pltpu.SMEM(doc_lengths.shape, jnp.int32),
            pltpu.VMEM((rows, cols), BF16),
            pltpu.VMEM((rows, cols), BF16),
            pltpu.VMEM((rows, state), BF16),
            pltpu.VMEM((rows, state), BF16),
            pltpu.VMEM((heads, rows), F32),
            pltpu.VMEM((1, heads), F32),
            pltpu.VMEM((1, heads), F32),
            pltpu.VMEM((1, cols), F32),
            pltpu.VMEM(queries.shape, BF16),
            pltpu.VMEM((slots, tok, 2 * kvw), BF16),
            pltpu.VMEM((chunks, state, width), BF16),
            pltpu.VMEM((chunks, state, width), BF16),
            pltpu.VMEM((chunks, state, width), F32),
            pltpu.VMEM((rows, cols), F32),
            pltpu.VMEM((4 * heads, cols), BF16),
            pltpu.VMEM((rows, 4 * heads), BF16),
            pltpu.VMEM((nt * (nt + 1) // 2, TILE, 4 * heads), BF16),
            pltpu.VMEM((16, 4 * heads), BF16),
            pltpu.VMEM((rows, rows), BF16),
            pltpu.VMEM((state, rows), BF16),
            pltpu.VMEM((rows, state), BF16),
            pltpu.VMEM((16, cols), F32),
            pltpu.VMEM((tok, slots * tok), F32),
            pltpu.VMEM((kvw // HEAD_D, tok * queries.shape[1] // kvw, HEAD_D), F32),
            pltpu.VMEM((kvw // HEAD_D, tok * queries.shape[1] // kvw, 1), F32),
            pltpu.VMEM((kvw // HEAD_D, tok * queries.shape[1] // kvw, 1), F32),
            dma((12,)),
            dma((slots,)),
            dma((2,)),
            dma((max(1, 4 * (nh - 1)),)),
            dma((chunks,)),
            dma((chunks,)),
        ],
        compiler_params=pltpu.CompilerParams(
            collective_id=0, has_side_effects=True, vmem_limit_bytes=60 * 1024 * 1024
        ),
    )(
        doc_lengths, ssm_input, ssm_gate, input_map, output_map, step_size, decay_log[None, :], skip_gain[None, :],
        norm_gain[None, :], queries, keys_in, values_in,
    )


def solution(mesh):
    channels = P(("groups", "seq"), ("head", "tp"))
    per_head = P(("head", "tp"))
    positions = P(("groups", "seq", "head"), "tp")
    return jax.shard_map(
        functools.partial(on_device, mesh.shape["seq"], mesh.shape["head"]),
        mesh=mesh,
        in_specs=(
            channels, channels, channels, channels, P(("head", "tp"), ("groups", "seq")), per_head, per_head, per_head,
            P("groups"), positions, positions, positions,
        ),
        out_specs=(channels, positions),
        check_vma=False,
    )
```

```python
import functools
import math

import jax
import jax.numpy as jnp
from jax import lax
from jax.experimental import pallas as pl
from jax.experimental.pallas import tpu as pltpu
from jax.sharding import PartitionSpec as P

HEAD_P = 64
HEAD_D = 128
REACH = 2
MESH = pl.DeviceIdType.MESH
TILE = 256
F32 = jnp.float32
BF16 = jnp.bfloat16


def dot(a, b):
    return jnp.dot(a, b, preferred_element_type=F32)


def dot_nt(a, b):
    return lax.dot_general(a, b, (((1,), (1,)), ((), ())), preferred_element_type=F32)


def split3(v):
    hi = v.astype(BF16).astype(F32)
    mid = (v - hi).astype(BF16).astype(F32)
    lo = (v - hi - mid).astype(BF16).astype(F32)
    return hi, mid, lo


def column(row, count):
    r = lax.broadcasted_iota(jnp.int32, (count, count), 0)
    c = lax.broadcasted_iota(jnp.int32, (count, count), 1)
    return jnp.sum(jnp.where(r == c, row, 0.0), axis=1, keepdims=True)


def stacked(v):
    hi, mid, lo = split3(v)
    return jnp.concatenate([hi, mid, lo, jnp.zeros_like(v)], axis=0).T.astype(BF16)


def kernel(
    nz, nh, width,
    dl_hbm, x_hbm, z_hbm, b_hbm, c_hbm, step_hbm, decay_hbm, skip_hbm, norm_hbm, q_hbm, k_hbm, v_hbm,
    so_ref, ao_ref,
    dl_ref, x_ref, z_ref, b_ref, c_ref, step_ref, decay_ref, skip_ref, norm_ref, q_ref,
    kv, s_in, s_out, local, pre, spread, e_parts, g_parts, row_parts, m_ref, bm_ref, cm_ref, rows_ref, bias_ref,
    mixed_ref, top_ref, sum_ref,
    loads, kv_recv, z_send, x_send, s_recv, s_send,
):
    z = lax.axis_index("seq")
    x = lax.axis_index("head")
    rows, cols = x_ref.shape
    heads = step_ref.shape[0]
    nt = rows // TILE
    chunks = cols // width
    tok = q_ref.shape[0]
    kvw = k_hbm.shape[1]
    slots = REACH * nh + 1
    own = slots - 1
    docs = dl_ref.shape[0]
    position = z * nh + x
    first = z * rows

    barrier = pltpu.get_barrier_semaphore()
    has_prev, has_next = z > 0, z < nz - 1

    def greet(axis, index):
        pl.semaphore_signal(barrier, inc=1, device_id={axis: index}, device_id_type=MESH)

    kv_heads = kvw // HEAD_D
    moves = []
    for g in range(kv_heads):
        for i, source in enumerate((k_hbm, v_hbm)):
            moves.append((
                source.at[:, pl.ds(g * HEAD_D, HEAD_D)], kv.at[own, g, :, pl.ds(i * HEAD_D, HEAD_D)]))
    early = len(moves)
    moves += [
        (step_hbm, step_ref),
        (decay_hbm, decay_ref), (skip_hbm, skip_ref), (dl_hbm, dl_ref), (b_hbm, b_ref), (c_hbm, c_ref), (x_hbm, x_ref),
        (q_hbm, q_ref), (z_hbm, z_ref), (norm_hbm, norm_ref),
    ]
    moves = [pltpu.make_async_copy(source, target, loads.at[i]) for i, (source, target) in enumerate(moves)]
    for move in moves:
        move.start()

    @pl.when(has_prev)
    def _():
        greet("seq", z - 1)

    @pl.when(has_next)
    def _():
        greet("seq", z + 1)

    for d in range(1, nh):
        greet("head", lax.rem(x + d, nh))

    pl.semaphore_wait(barrier, has_prev.astype(jnp.int32) + has_next.astype(jnp.int32) + nh - 1)

    for move in moves[:early]:
        move.wait()

    def to_next(source, target, sem, g):
        return pltpu.make_async_remote_copy(
            src_ref=kv.at[source, g], dst_ref=kv.at[target, g], send_sem=z_send.at[sem, g],
            recv_sem=kv_recv.at[target, g], device_id={"seq": z + 1}, device_id_type=MESH)

    def to_side(source, target, sem, peer, g):
        return pltpu.make_async_remote_copy(
            src_ref=kv.at[source, g], dst_ref=kv.at[target, g], send_sem=x_send.at[sem, g],
            recv_sem=kv_recv.at[target, g], device_id={"head": peer}, device_id_type=MESH)

    def side_copies(d, g):
        up, down = x + d < nh, x - d >= 0
        base = (d - 1) * 4
        return {
            0: [(up, lambda: to_side(own, own - d, base, x + d, g))],
            1: [
                (up & has_prev, lambda: to_side(nh, nh - d, base + 1, x + d, g)),
                (down & has_prev, lambda: to_side(nh, nh + d, base + 2, x - d, g)),
            ],
            2: [(down & (z > 1), lambda: to_side(0, d, base + 3, x - d, g))],
        }

    def start_stage(stage, g):
        for d in range(1, nh):
            for exists, make in side_copies(d, g)[stage]:
                pl.when(exists)(lambda make=make: make().start())

    def arrived(slot, g):
        pltpu.make_async_copy(kv.at[slot, g], kv.at[slot, g], kv_recv.at[slot, g]).wait()

    def send_own(g, _):
        pl.when(has_next)(lambda: to_next(own, nh, 0, g).start())
        start_stage(0, g)
        return 0

    lax.fori_loop(0, kv_heads, send_own, 0)

    for slot in range(own):
        @pl.when(position - own + slot < 0)
        def _():
            kv[slot] = jnp.zeros(kv.shape[1:], BF16)

    @pl.when(z == 0)
    def _():
        s_in[...] = jnp.zeros_like(s_in)

    for move in moves[early : early + 6]:
        move.wait()

    def doc_start(pos):
        best = jnp.zeros_like(pos)
        start = jnp.int32(0)
        for d in range(docs):
            best = jnp.where(start <= pos, jnp.maximum(best, start), best)
            start = start + dl_ref[d]
        return best

    end_start = doc_start(first + rows - 1)
    rates = column(-jnp.exp(decay_ref[...]), heads)
    step = step_ref[...]
    s_iota = lax.broadcasted_iota(jnp.int32, (rows, rows), 0)
    t_iota = lax.broadcasted_iota(jnp.int32, (rows, rows), 1)
    upper = jnp.where(s_iota <= t_iota, 1.0, 0.0).astype(BF16)
    hi, mid, lo = split3(step * rates)
    cum = dot(hi.astype(BF16), upper) + dot(mid.astype(BF16), upper) + dot(lo.astype(BF16), upper)
    last = cum[:, rows - 1 : rows]
    factor = jnp.where(end_start >= first, 0.0, jnp.exp(last))
    lane = lax.broadcasted_iota(jnp.int32, (heads, 128), 1)
    table = jnp.where(lane == 0, factor, jnp.where(lane == 1, column(skip_ref[...], heads), 0.0))
    pair = 0
    for i in range(nt):
        mark = i * TILE + TILE // 2 - 1
        ref = cum[:, mark : mark + 1]
        table = jnp.where(lane == 2 + 2 * i, jnp.exp(ref), table)
        table = jnp.where(lane == 3 + 2 * i, jnp.exp(last - ref), table)
        here = slice(i * TILE, (i + 1) * TILE)
        e_parts[here, :] = stacked(jnp.exp(cum[:, here] - ref))
        for j in range(i + 1):
            there = slice(j * TILE, (j + 1) * TILE)
            g_parts[pair] = stacked(jnp.exp(ref - cum[:, there]) * step[:, there])
            pair += 1
    row_parts[...] = stacked(table)[:16]
    r_iota = lax.broadcasted_iota(jnp.int32, spread.shape, 0)
    h_iota = lax.broadcasted_iota(jnp.int32, spread.shape, 1) // HEAD_P
    hit = r_iota == h_iota
    for piece in range(1, 4):
        hit = hit | (r_iota == h_iota + piece * heads)
    spread[...] = jnp.where(hit, 1.0, 0.0).astype(BF16)
    rows_ref[...] = dot(row_parts[...], spread[...])

    pos_t = first + lax.broadcasted_iota(jnp.int32, (rows, 1), 0)
    start_t = doc_start(pos_t)
    pos_s = first + lax.broadcasted_iota(jnp.int32, (rows, rows), 1)
    inter = dot_nt(c_ref[...], b_ref[...])
    m_ref[...] = jnp.where((pos_s >= start_t) & (pos_s <= pos_t), inter, 0.0).astype(BF16)
    bm_ref[...] = jnp.where(pos_t >= end_start, b_ref[...].astype(F32), 0.0).T.astype(BF16)
    cm_ref[...] = jnp.where(start_t < first, c_ref[...].astype(F32), 0.0).astype(BF16)
    query_t = position * tok + lax.broadcasted_iota(jnp.int32, (tok, 1), 0)
    key_s = (position - own) * tok + lax.broadcasted_iota(jnp.int32, (tok, slots * tok), 1)
    bias_ref[...] = jnp.where((key_s >= doc_start(query_t)) & (key_s <= query_t), 0.0, -jnp.inf)

    def state_copy(c):
        return pltpu.make_async_remote_copy(
            src_ref=s_out.at[c], dst_ref=s_in.at[c], send_sem=s_send.at[c], recv_sem=s_recv.at[c],
            device_id={"seq": z + 1}, device_id_type=MESH)

    def chunk_of(c):
        return pl.ds(pl.multiple_of(c * width, width), width)

    def block_part(c, _):
        at = chunk_of(c)
        state = jnp.zeros((bm_ref.shape[0], width), F32)
        pair = 0
        for i in range(nt):
            here = slice(i * TILE, (i + 1) * TILE)
            total = jnp.zeros((TILE, width), F32)
            for j in range(i + 1):
                there = slice(j * TILE, (j + 1) * TILE)
                scaled = (dot(g_parts[pair], spread[:, at]) * x_ref[there, at].astype(F32)).astype(BF16)
                total += dot(m_ref[here, there], scaled)
                pair += 1
            pre[here, at] = total
            state += dot(bm_ref[:, here], scaled) * rows_ref[3 + 2 * i : 4 + 2 * i, at]
        local[c] = state

        @pl.when(z == 0)
        def _():
            s_out[c] = state.astype(BF16)
            if nz > 1:
                state_copy(c).start()
        return 0

    moves[early + 6].wait()
    lax.fori_loop(0, chunks, block_part, 0)
    for move in moves[early + 7 :]:
        move.wait()

    def relay(g, _):
        @pl.when(has_prev)
        def _():
            arrived(nh, g)
            pl.when(has_next)(lambda: to_next(nh, 0, 1, g).start())

        start_stage(1, g)
        return 0

    lax.fori_loop(0, kv_heads, relay, 0)

    group = q_hbm.shape[1] // kvw
    scale = 1.0 / math.sqrt(HEAD_D)

    def head_at(start):
        return pl.ds(pl.multiple_of(start, HEAD_D), HEAD_D)

    def logits_of(g, low, high):
        query = jnp.concatenate([q_ref[:, head_at((g * group + j) * HEAD_D)] for j in range(group)], axis=0)
        key = jnp.concatenate([kv[s, g, :, :HEAD_D] for s in range(low, high)], axis=0)
        value = jnp.concatenate([kv[s, g, :, HEAD_D:] for s in range(low, high)], axis=0)
        bias = jnp.concatenate([bias_ref[:, low * tok : high * tok]] * group, axis=0)
        return dot_nt(query, key) * scale + bias, value

    def near(g):
        for slot in range(nh + 1, own):
            pl.when(position - own + slot >= 0)(lambda slot=slot: arrived(slot, g))
        logits, value = logits_of(g, nh, slots)
        top = jnp.max(logits, axis=1, keepdims=True)
        probs = jnp.exp(logits - top)
        mixed_ref[g] = dot(probs.astype(BF16), value)
        top_ref[g] = top
        sum_ref[g] = jnp.sum(probs, axis=1, keepdims=True)

    def far(g):
        for slot in range(1, nh):
            pl.when(position - own + slot >= 0)(lambda slot=slot: arrived(slot, g))
        logits, value = logits_of(g, 0, nh)
        before = top_ref[g]
        top = jnp.maximum(before, jnp.max(logits, axis=1, keepdims=True))
        probs = jnp.exp(logits - top)
        keep = jnp.exp(before - top)
        total = jnp.sum(probs, axis=1, keepdims=True) + sum_ref[g] * keep
        mixed = (dot(probs.astype(BF16), value) + mixed_ref[g] * keep) / total
        for j in range(group):
            ao_ref[:, head_at((g * group + j) * HEAD_D)] = mixed[j * tok : (j + 1) * tok].astype(BF16)

    def state_part(c, squares):
        at = chunk_of(c)

        @pl.when(has_prev)
        def _():
            pltpu.make_async_copy(s_in.at[c], s_in.at[c], s_recv.at[c]).wait()

            @pl.when(has_next)
            def _():
                s_out[c] = (local[c] + rows_ref[0:1, at] * s_in[c].astype(F32)).astype(BF16)
                state_copy(c).start()

        inbound = s_in[c].astype(F32)
        sums = []
        for i in range(nt):
            here = slice(i * TILE, (i + 1) * TILE)
            scaled = (inbound * rows_ref[2 + 2 * i : 3 + 2 * i, at]).astype(BF16)
            total = (pre[here, at] + dot(cm_ref[here, :], scaled)) * dot(e_parts[here, :], spread[:, at])
            total += rows_ref[1:2, at] * x_ref[here, at].astype(F32)
            gate = z_ref[here, at].astype(F32)
            gated = total * (gate / (1.0 + jnp.exp(-gate)))
            pre[here, at] = gated
            sums.append(jnp.sum(gated * gated, axis=1, keepdims=True))
        return squares + jnp.concatenate(sums, axis=0)

    def far_start(g):
        pl.when(z > 1)(lambda: arrived(0, g))
        start_stage(2, g)

    def step_part(c, squares):
        near_g, start_g, far_g = c, c, c - (chunks - kv_heads)
        pl.when((far_g >= 0) & (far_g < kv_heads) )(lambda: far(far_g))
        pl.when((start_g >= 0) & (start_g < kv_heads))(lambda: far_start(start_g))
        squares = state_part(c, squares)
        pl.when((near_g >= 0) & (near_g < kv_heads))(lambda: near(near_g))
        return squares

    at_end = z == nz - 1
    squares = lax.fori_loop(0, chunks, step_part, jnp.zeros((rows, 1), F32))
    inverse = lax.rsqrt(squares * (1.0 / cols) + 1e-05)

    def norm_part(c, _):
        at = chunk_of(c)
        so_ref[:, at] = (pre[:, at] * inverse * norm_ref[:, at]).astype(BF16)
        return 0

    lax.fori_loop(0, chunks, norm_part, 0)


    @pl.when(has_next)
    def _():
        def passed(g, _):
            to_next(own, nh, 0, g).wait_send()
            pl.when(has_prev)(lambda: to_next(nh, 0, 1, g).wait_send())
            return 0

        lax.fori_loop(0, kv_heads, passed, 0)

        def sent(c, _):
            state_copy(c).wait_send()
            return 0

        lax.fori_loop(0, chunks, sent, 0)

    def side_passed(g, _):
        for d in range(1, nh):
            for copies in side_copies(d, g).values():
                for exists, make in copies:
                    pl.when(exists)(lambda make=make: make().wait_send())
        return 0

    lax.fori_loop(0, kv_heads, side_passed, 0)


def on_device(
    nz, nh,
    ssm_input, ssm_gate, input_map, output_map, step_size, decay_log, skip_gain, norm_gain, doc_lengths,
    queries, keys_in, values_in,
):
    rows, cols = ssm_input.shape
    heads = step_size.shape[0]
    state = input_map.shape[1]
    tok, kvw = keys_in.shape
    width = cols // 8
    chunks = cols // width
    nt = rows // TILE
    slots = REACH * nh + 1
    vmem = pl.BlockSpec(memory_space=pltpu.VMEM)
    dma = pltpu.SemaphoreType.DMA
    return pl.pallas_call(
        functools.partial(kernel, nz, nh, width),
        out_shape=(
            jax.ShapeDtypeStruct((rows, cols), BF16),
            jax.ShapeDtypeStruct(queries.shape, BF16),
        ),
        in_specs=[pl.BlockSpec(memory_space=pltpu.HBM)] * 12,
        out_specs=(vmem, vmem),
        scratch_shapes=[
            pltpu.SMEM(doc_lengths.shape, jnp.int32),
            pltpu.VMEM((rows, cols), BF16),
            pltpu.VMEM((rows, cols), BF16),
            pltpu.VMEM((rows, state), BF16),
            pltpu.VMEM((rows, state), BF16),
            pltpu.VMEM((heads, rows), F32),
            pltpu.VMEM((1, heads), F32),
            pltpu.VMEM((1, heads), F32),
            pltpu.VMEM((1, cols), F32),
            pltpu.VMEM(queries.shape, BF16),
            pltpu.VMEM((slots, kvw // HEAD_D, tok, 2 * HEAD_D), BF16),
            pltpu.VMEM((chunks, state, width), BF16),
            pltpu.VMEM((chunks, state, width), BF16),
            pltpu.VMEM((chunks, state, width), F32),
            pltpu.VMEM((rows, cols), F32),
            pltpu.VMEM((4 * heads, cols), BF16),
            pltpu.VMEM((rows, 4 * heads), BF16),
            pltpu.VMEM((nt * (nt + 1) // 2, TILE, 4 * heads), BF16),
            pltpu.VMEM((16, 4 * heads), BF16),
            pltpu.VMEM((rows, rows), BF16),
            pltpu.VMEM((state, rows), BF16),
            pltpu.VMEM((rows, state), BF16),
            pltpu.VMEM((16, cols), F32),
            pltpu.VMEM((tok, slots * tok), F32),
            pltpu.VMEM((kvw // HEAD_D, tok * queries.shape[1] // kvw, HEAD_D), F32),
            pltpu.VMEM((kvw // HEAD_D, tok * queries.shape[1] // kvw, 1), F32),
            pltpu.VMEM((kvw // HEAD_D, tok * queries.shape[1] // kvw, 1), F32),
            dma((10 + 2 * (kvw // HEAD_D),)),
            dma((slots, kvw // HEAD_D)),
            dma((2, kvw // HEAD_D)),
            dma((max(1, 4 * (nh - 1)), kvw // HEAD_D)),
            dma((chunks,)),
            dma((chunks,)),
        ],
        compiler_params=pltpu.CompilerParams(
            collective_id=0, has_side_effects=True, vmem_limit_bytes=60 * 1024 * 1024
        ),
    )(
        doc_lengths, ssm_input, ssm_gate, input_map, output_map, step_size, decay_log[None, :], skip_gain[None, :],
        norm_gain[None, :], queries, keys_in, values_in,
    )


def solution(mesh):
    channels = P(("groups", "seq"), ("head", "tp"))
    per_head = P(("head", "tp"))
    positions = P(("groups", "seq", "head"), "tp")
    return jax.shard_map(
        functools.partial(on_device, mesh.shape["seq"], mesh.shape["head"]),
        mesh=mesh,
        in_specs=(
            channels, channels, channels, channels, P(("head", "tp"), ("groups", "seq")), per_head, per_head, per_head,
            P("groups"), positions, positions, positions,
        ),
        out_specs=(channels, positions),
        check_vma=False,
    )
```

```python
import functools
import math

import jax
import jax.numpy as jnp
from jax import lax
from jax.experimental import pallas as pl
from jax.experimental.pallas import tpu as pltpu
from jax.sharding import PartitionSpec as P

HEAD_P = 64
HEAD_D = 128
REACH = 2
MESH = pl.DeviceIdType.MESH
TILE = 256
F32 = jnp.float32
BF16 = jnp.bfloat16


def dot(a, b):
    return jnp.dot(a, b, preferred_element_type=F32)


def dot_nt(a, b):
    return lax.dot_general(a, b, (((1,), (1,)), ((), ())), preferred_element_type=F32)


def split3(v):
    hi = v.astype(BF16).astype(F32)
    mid = (v - hi).astype(BF16).astype(F32)
    lo = (v - hi - mid).astype(BF16).astype(F32)
    return hi, mid, lo


def column(row, count):
    r = lax.broadcasted_iota(jnp.int32, (count, count), 0)
    c = lax.broadcasted_iota(jnp.int32, (count, count), 1)
    return jnp.sum(jnp.where(r == c, row, 0.0), axis=1, keepdims=True)


def stacked(v):
    hi, mid, lo = split3(v)
    return jnp.concatenate([hi, mid, lo, jnp.zeros_like(v)], axis=0).T.astype(BF16)


def kernel(
    nz, nh, width,
    dl_hbm, x_hbm, z_hbm, b_hbm, c_hbm, step_hbm, decay_hbm, skip_hbm, norm_hbm, q_hbm, k_hbm, v_hbm,
    so_hbm, ao_hbm,
    so_ref, ao_ref, dl_ref, x_ref, z_ref, b_ref, c_ref, step_ref, decay_ref, skip_ref, norm_ref, q_ref,
    kv, s_in, s_out, local, pre, spread, e_parts, g_parts, row_parts, m_ref, bm_ref, cm_ref, rows_ref, bias_ref,
    mixed_ref, top_ref, sum_ref,
    loads, so_done, ao_done, kv_recv, z_send, x_send, s_recv, s_send,
):
    z = lax.axis_index("seq")
    x = lax.axis_index("head")
    rows, cols = x_ref.shape
    heads = step_ref.shape[0]
    nt = rows // TILE
    chunks = cols // width
    tok = q_ref.shape[0]
    kvw = k_hbm.shape[1]
    slots = REACH * nh + 1
    own = slots - 1
    docs = dl_ref.shape[0]
    position = z * nh + x
    first = z * rows

    barrier = pltpu.get_barrier_semaphore()
    has_prev, has_next = z > 0, z < nz - 1

    def greet(axis, index):
        pl.semaphore_signal(barrier, inc=1, device_id={axis: index}, device_id_type=MESH)

    kv_heads = kvw // HEAD_D
    moves = []
    for g in range(kv_heads):
        for i, source in enumerate((k_hbm, v_hbm)):
            moves.append((
                source.at[:, pl.ds(g * HEAD_D, HEAD_D)], kv.at[own, g, :, pl.ds(i * HEAD_D, HEAD_D)]))
    early = len(moves)
    moves += [
        (step_hbm, step_ref),
        (decay_hbm, decay_ref), (skip_hbm, skip_ref), (dl_hbm, dl_ref), (b_hbm, b_ref), (c_hbm, c_ref), (x_hbm, x_ref),
        (q_hbm, q_ref), (z_hbm, z_ref), (norm_hbm, norm_ref),
    ]
    moves = [pltpu.make_async_copy(source, target, loads.at[i]) for i, (source, target) in enumerate(moves)]
    for move in moves:
        move.start()

    @pl.when(has_prev)
    def _():
        greet("seq", z - 1)

    @pl.when(has_next)
    def _():
        greet("seq", z + 1)

    for d in range(1, nh):
        greet("head", lax.rem(x + d, nh))

    pl.semaphore_wait(barrier, has_prev.astype(jnp.int32) + has_next.astype(jnp.int32) + nh - 1)

    for move in moves[:early]:
        move.wait()

    def to_next(source, target, sem, g):
        return pltpu.make_async_remote_copy(
            src_ref=kv.at[source, g], dst_ref=kv.at[target, g], send_sem=z_send.at[sem, g],
            recv_sem=kv_recv.at[target, g], device_id={"seq": z + 1}, device_id_type=MESH)

    def to_side(source, target, sem, peer, g):
        return pltpu.make_async_remote_copy(
            src_ref=kv.at[source, g], dst_ref=kv.at[target, g], send_sem=x_send.at[sem, g],
            recv_sem=kv_recv.at[target, g], device_id={"head": peer}, device_id_type=MESH)

    def side_copies(d, g):
        up, down = x + d < nh, x - d >= 0
        base = (d - 1) * 4
        return {
            0: [(up, lambda: to_side(own, own - d, base, x + d, g))],
            1: [
                (up & has_prev, lambda: to_side(nh, nh - d, base + 1, x + d, g)),
                (down & has_prev, lambda: to_side(nh, nh + d, base + 2, x - d, g)),
            ],
            2: [(down & (z > 1), lambda: to_side(0, d, base + 3, x - d, g))],
        }

    def start_stage(stage, g):
        for d in range(1, nh):
            for exists, make in side_copies(d, g)[stage]:
                pl.when(exists)(lambda make=make: make().start())

    def arrived(slot, g):
        pltpu.make_async_copy(kv.at[slot, g], kv.at[slot, g], kv_recv.at[slot, g]).wait()

    def send_own(g, _):
        pl.when(has_next)(lambda: to_next(own, nh, 0, g).start())
        start_stage(0, g)
        return 0

    lax.fori_loop(0, kv_heads, send_own, 0)

    for slot in range(own):
        @pl.when(position - own + slot < 0)
        def _():
            kv[slot] = jnp.zeros(kv.shape[1:], BF16)

    @pl.when(z == 0)
    def _():
        s_in[...] = jnp.zeros_like(s_in)

    for move in moves[early : early + 6]:
        move.wait()

    def doc_start(pos):
        best = jnp.zeros_like(pos)
        start = jnp.int32(0)
        for d in range(docs):
            best = jnp.where(start <= pos, jnp.maximum(best, start), best)
            start = start + dl_ref[d]
        return best

    end_start = doc_start(first + rows - 1)
    rates = column(-jnp.exp(decay_ref[...]), heads)
    step = step_ref[...]
    s_iota = lax.broadcasted_iota(jnp.int32, (rows, rows), 0)
    t_iota = lax.broadcasted_iota(jnp.int32, (rows, rows), 1)
    upper = jnp.where(s_iota <= t_iota, 1.0, 0.0).astype(BF16)
    hi, mid, lo = split3(step * rates)
    cum = dot(hi.astype(BF16), upper) + dot(mid.astype(BF16), upper) + dot(lo.astype(BF16), upper)
    last = cum[:, rows - 1 : rows]
    factor = jnp.where(end_start >= first, 0.0, jnp.exp(last))
    lane = lax.broadcasted_iota(jnp.int32, (heads, 128), 1)
    table = jnp.where(lane == 0, factor, jnp.where(lane == 1, column(skip_ref[...], heads), 0.0))
    pair = 0
    for i in range(nt):
        mark = i * TILE + TILE // 2 - 1
        ref = cum[:, mark : mark + 1]
        table = jnp.where(lane == 2 + 2 * i, jnp.exp(ref), table)
        table = jnp.where(lane == 3 + 2 * i, jnp.exp(last - ref), table)
        here = slice(i * TILE, (i + 1) * TILE)
        e_parts[here, :] = stacked(jnp.exp(cum[:, here] - ref))
        for j in range(i + 1):
            there = slice(j * TILE, (j + 1) * TILE)
            g_parts[pair] = stacked(jnp.exp(ref - cum[:, there]) * step[:, there])
            pair += 1
    row_parts[...] = stacked(table)[:16]
    r_iota = lax.broadcasted_iota(jnp.int32, spread.shape, 0)
    h_iota = lax.broadcasted_iota(jnp.int32, spread.shape, 1) // HEAD_P
    hit = r_iota == h_iota
    for piece in range(1, 4):
        hit = hit | (r_iota == h_iota + piece * heads)
    spread[...] = jnp.where(hit, 1.0, 0.0).astype(BF16)
    rows_ref[...] = dot(row_parts[...], spread[...])

    pos_t = first + lax.broadcasted_iota(jnp.int32, (rows, 1), 0)
    start_t = doc_start(pos_t)
    pos_s = first + lax.broadcasted_iota(jnp.int32, (rows, rows), 1)
    inter = dot_nt(c_ref[...], b_ref[...])
    m_ref[...] = jnp.where((pos_s >= start_t) & (pos_s <= pos_t), inter, 0.0).astype(BF16)
    bm_ref[...] = jnp.where(pos_t >= end_start, b_ref[...].astype(F32), 0.0).T.astype(BF16)
    cm_ref[...] = jnp.where(start_t < first, c_ref[...].astype(F32), 0.0).astype(BF16)
    query_t = position * tok + lax.broadcasted_iota(jnp.int32, (tok, 1), 0)
    key_s = (position - own) * tok + lax.broadcasted_iota(jnp.int32, (tok, slots * tok), 1)
    bias_ref[...] = jnp.where((key_s >= doc_start(query_t)) & (key_s <= query_t), 0.0, -jnp.inf)

    def state_copy(c):
        return pltpu.make_async_remote_copy(
            src_ref=s_out.at[c], dst_ref=s_in.at[c], send_sem=s_send.at[c], recv_sem=s_recv.at[c],
            device_id={"seq": z + 1}, device_id_type=MESH)

    def chunk_of(c):
        return pl.ds(pl.multiple_of(c * width, width), width)

    def block_part(c, _):
        at = chunk_of(c)
        state = jnp.zeros((bm_ref.shape[0], width), F32)
        pair = 0
        for i in range(nt):
            here = slice(i * TILE, (i + 1) * TILE)
            total = jnp.zeros((TILE, width), F32)
            for j in range(i + 1):
                there = slice(j * TILE, (j + 1) * TILE)
                scaled = (dot(g_parts[pair], spread[:, at]) * x_ref[there, at].astype(F32)).astype(BF16)
                total += dot(m_ref[here, there], scaled)
                pair += 1
            pre[here, at] = total
            state += dot(bm_ref[:, here], scaled) * rows_ref[3 + 2 * i : 4 + 2 * i, at]
        local[c] = state

        @pl.when(z == 0)
        def _():
            s_out[c] = state.astype(BF16)
            if nz > 1:
                state_copy(c).start()
        return 0

    moves[early + 6].wait()
    lax.fori_loop(0, chunks, block_part, 0)
    for move in moves[early + 7 :]:
        move.wait()

    def relay(g, _):
        @pl.when(has_prev)
        def _():
            arrived(nh, g)
            pl.when(has_next)(lambda: to_next(nh, 0, 1, g).start())

        start_stage(1, g)
        return 0

    lax.fori_loop(0, kv_heads, relay, 0)

    group = q_hbm.shape[1] // kvw
    scale = 1.0 / math.sqrt(HEAD_D)

    def head_at(start):
        return pl.ds(pl.multiple_of(start, HEAD_D), HEAD_D)

    def logits_of(g, low, high):
        query = jnp.concatenate([q_ref[:, head_at((g * group + j) * HEAD_D)] for j in range(group)], axis=0)
        key = jnp.concatenate([kv[s, g, :, :HEAD_D] for s in range(low, high)], axis=0)
        value = jnp.concatenate([kv[s, g, :, HEAD_D:] for s in range(low, high)], axis=0)
        bias = jnp.concatenate([bias_ref[:, low * tok : high * tok]] * group, axis=0)
        return dot_nt(query, key) * scale + bias, value

    def so_copy(c):
        return pltpu.make_async_copy(so_ref.at[:, chunk_of(c)], so_hbm.at[:, chunk_of(c)], so_done.at[c])

    def ao_copy(g):
        at = pl.ds(pl.multiple_of(g * group * HEAD_D, HEAD_D), group * HEAD_D)
        return pltpu.make_async_copy(ao_ref.at[:, at], ao_hbm.at[:, at], ao_done.at[g])

    def near(g):
        for slot in range(nh + 1, own):
            pl.when(position - own + slot >= 0)(lambda slot=slot: arrived(slot, g))
        logits, value = logits_of(g, nh, slots)
        top = jnp.max(logits, axis=1, keepdims=True)
        probs = jnp.exp(logits - top)
        mixed_ref[g] = dot(probs.astype(BF16), value)
        top_ref[g] = top
        sum_ref[g] = jnp.sum(probs, axis=1, keepdims=True)

    def far(g):
        for slot in range(1, nh):
            pl.when(position - own + slot >= 0)(lambda slot=slot: arrived(slot, g))
        logits, value = logits_of(g, 0, nh)
        before = top_ref[g]
        top = jnp.maximum(before, jnp.max(logits, axis=1, keepdims=True))
        probs = jnp.exp(logits - top)
        keep = jnp.exp(before - top)
        total = jnp.sum(probs, axis=1, keepdims=True) + sum_ref[g] * keep
        mixed = (dot(probs.astype(BF16), value) + mixed_ref[g] * keep) / total
        for j in range(group):
            ao_ref[:, head_at((g * group + j) * HEAD_D)] = mixed[j * tok : (j + 1) * tok].astype(BF16)
        ao_copy(g).start()

    def state_part(c, squares):
        at = chunk_of(c)

        @pl.when(has_prev)
        def _():
            pltpu.make_async_copy(s_in.at[c], s_in.at[c], s_recv.at[c]).wait()

            @pl.when(has_next)
            def _():
                s_out[c] = (local[c] + rows_ref[0:1, at] * s_in[c].astype(F32)).astype(BF16)
                state_copy(c).start()

        inbound = s_in[c].astype(F32)
        sums = []
        for i in range(nt):
            here = slice(i * TILE, (i + 1) * TILE)
            scaled = (inbound * rows_ref[2 + 2 * i : 3 + 2 * i, at]).astype(BF16)
            total = (pre[here, at] + dot(cm_ref[here, :], scaled)) * dot(e_parts[here, :], spread[:, at])
            total += rows_ref[1:2, at] * x_ref[here, at].astype(F32)
            gate = z_ref[here, at].astype(F32)
            gated = total * (gate / (1.0 + jnp.exp(-gate)))
            pre[here, at] = gated
            sums.append(jnp.sum(gated * gated, axis=1, keepdims=True))
        return squares + jnp.concatenate(sums, axis=0)

    def far_start(g):
        pl.when(z > 1)(lambda: arrived(0, g))
        start_stage(2, g)

    def step_part(c, squares):
        near_g, far_g = c, c - (chunks - kv_heads)
        pl.when((far_g >= 0) & (far_g < kv_heads) )(lambda: far(far_g))
        squares = state_part(c, squares)
        pl.when((near_g >= 0) & (near_g < kv_heads))(lambda: near(near_g))
        return squares

    at_end = z == nz - 1

    def start_part(g, _):
        far_start(g)
        return 0

    lax.fori_loop(0, kv_heads, start_part, 0)
    squares = lax.fori_loop(0, chunks, step_part, jnp.zeros((rows, 1), F32))
    inverse = lax.rsqrt(squares * (1.0 / cols) + 1e-05)

    def norm_part(c, _):
        at = chunk_of(c)
        so_ref[:, at] = (pre[:, at] * inverse * norm_ref[:, at]).astype(BF16)
        so_copy(c).start()
        return 0

    lax.fori_loop(0, chunks, norm_part, 0)


    def so_left(c, _):
        so_copy(c).wait()
        return 0

    def ao_left(g, _):
        ao_copy(g).wait()
        return 0

    lax.fori_loop(0, chunks, so_left, 0)
    lax.fori_loop(0, kv_heads, ao_left, 0)

    @pl.when(has_next)
    def _():
        def passed(g, _):
            to_next(own, nh, 0, g).wait_send()
            pl.when(has_prev)(lambda: to_next(nh, 0, 1, g).wait_send())
            return 0

        lax.fori_loop(0, kv_heads, passed, 0)

        def sent(c, _):
            state_copy(c).wait_send()
            return 0

        lax.fori_loop(0, chunks, sent, 0)

    def side_passed(g, _):
        for d in range(1, nh):
            for copies in side_copies(d, g).values():
                for exists, make in copies:
                    pl.when(exists)(lambda make=make: make().wait_send())
        return 0

    lax.fori_loop(0, kv_heads, side_passed, 0)


def on_device(
    nz, nh,
    ssm_input, ssm_gate, input_map, output_map, step_size, decay_log, skip_gain, norm_gain, doc_lengths,
    queries, keys_in, values_in,
):
    rows, cols = ssm_input.shape
    heads = step_size.shape[0]
    state = input_map.shape[1]
    tok, kvw = keys_in.shape
    width = cols // 8
    chunks = cols // width
    nt = rows // TILE
    slots = REACH * nh + 1
    dma = pltpu.SemaphoreType.DMA
    return pl.pallas_call(
        functools.partial(kernel, nz, nh, width),
        out_shape=(
            jax.ShapeDtypeStruct((rows, cols), BF16),
            jax.ShapeDtypeStruct(queries.shape, BF16),
        ),
        in_specs=[pl.BlockSpec(memory_space=pltpu.HBM)] * 12,
        out_specs=(pl.BlockSpec(memory_space=pltpu.HBM),) * 2,
        scratch_shapes=[
            pltpu.VMEM((rows, cols), BF16),
            pltpu.VMEM(queries.shape, BF16),
            pltpu.SMEM(doc_lengths.shape, jnp.int32),
            pltpu.VMEM((rows, cols), BF16),
            pltpu.VMEM((rows, cols), BF16),
            pltpu.VMEM((rows, state), BF16),
            pltpu.VMEM((rows, state), BF16),
            pltpu.VMEM((heads, rows), F32),
            pltpu.VMEM((1, heads), F32),
            pltpu.VMEM((1, heads), F32),
            pltpu.VMEM((1, cols), F32),
            pltpu.VMEM(queries.shape, BF16),
            pltpu.VMEM((slots, kvw // HEAD_D, tok, 2 * HEAD_D), BF16),
            pltpu.VMEM((chunks, state, width), BF16),
            pltpu.VMEM((chunks, state, width), BF16),
            pltpu.VMEM((chunks, state, width), F32),
            pltpu.VMEM((rows, cols), F32),
            pltpu.VMEM((4 * heads, cols), BF16),
            pltpu.VMEM((rows, 4 * heads), BF16),
            pltpu.VMEM((nt * (nt + 1) // 2, TILE, 4 * heads), BF16),
            pltpu.VMEM((16, 4 * heads), BF16),
            pltpu.VMEM((rows, rows), BF16),
            pltpu.VMEM((state, rows), BF16),
            pltpu.VMEM((rows, state), BF16),
            pltpu.VMEM((16, cols), F32),
            pltpu.VMEM((tok, slots * tok), F32),
            pltpu.VMEM((kvw // HEAD_D, tok * queries.shape[1] // kvw, HEAD_D), F32),
            pltpu.VMEM((kvw // HEAD_D, tok * queries.shape[1] // kvw, 1), F32),
            pltpu.VMEM((kvw // HEAD_D, tok * queries.shape[1] // kvw, 1), F32),
            dma((10 + 2 * (kvw // HEAD_D),)),
            dma((chunks,)),
            dma((kvw // HEAD_D,)),
            dma((slots, kvw // HEAD_D)),
            dma((2, kvw // HEAD_D)),
            dma((max(1, 4 * (nh - 1)), kvw // HEAD_D)),
            dma((chunks,)),
            dma((chunks,)),
        ],
        compiler_params=pltpu.CompilerParams(
            collective_id=0, has_side_effects=True, vmem_limit_bytes=60 * 1024 * 1024
        ),
    )(
        doc_lengths, ssm_input, ssm_gate, input_map, output_map, step_size, decay_log[None, :], skip_gain[None, :],
        norm_gain[None, :], queries, keys_in, values_in,
    )


def solution(mesh):
    channels = P(("groups", "seq"), ("head", "tp"))
    per_head = P(("head", "tp"))
    positions = P(("groups", "seq", "head"), "tp")
    return jax.shard_map(
        functools.partial(on_device, mesh.shape["seq"], mesh.shape["head"]),
        mesh=mesh,
        in_specs=(
            channels, channels, channels, channels, P(("head", "tp"), ("groups", "seq")), per_head, per_head, per_head,
            P("groups"), positions, positions, positions,
        ),
        out_specs=(channels, positions),
        check_vma=False,
    )
```
